768 devices in a mesh: row: 16 (over y, core), col: 12 (over z_lo, x), split: 4 (over z_hi).
Axes of the slice: x: 4, y: 8, z: 12 (z_hi: 4, z_lo: 3; z = z_hi * 3 + z_lo), core: 2. Of those that a mesh axis runs over, the one named last changes fastest.
Arguments:
- start_vectors: float32 [8, 98304], P(None, ('row', 'col', 'split')), may hold values from -16 to 16
- diag_energy: float32 [98304], P(('row', 'col', 'split')), may hold values from 0.35 to 6
- matrix_blocks: float32 [16, 12, 64, 128, 128], P('row', 'col', 'split'), may hold values from -0.125 to 0.125
- block_rows: int32 [16, 12, 64], P('row', 'col', 'split'), may hold values from 0 to 47, as said below
- block_cols: int32 [16, 12, 64], P('row', 'col', 'split'), may hold values from 0 to 63
- counts: int32 [16, 12, 4], P('row', 'col', 'split'), may hold values from 0 to 16, as said below
Outputs:
- residual_block: float32 [8, 98304], P(None, ('row', 'col', 'split'))
- second_image: float32 [8, 98304], P(None, ('row', 'col', 'split'))
The draws below stay inside these ranges and needn't reach their ends.
Inputs may be any that keep to these rules, and one draw needn't show every extreme that they name: `block_rows`: every used slot names a block strictly above the block diagonal in the global numbering; slots at or past the count are unused and their entries are arbitrary within range. `counts`: some tile split holds exactly 16 used slots in every draw.
All inputs are finite; a program needn't handle non-finite values.
Results may differ from the reference program's by a relative error of at most 0.0003.
Values sent between devices are 32-bit elements; how exact they have to be, the bound alone decides.
No kernel may reach another device: no remote copies, remote signals or barrier semaphores. Data moves between devices by JAX's collectives and lax.ppermute only.
A program may use at most 32 MiB of HBM per device.

```python
import jax
import jax.numpy as jnp
from jax import lax

BS = 128
NV = 8
VR = 128
MAXB = 16
SLOTS = 64
RB = 48
ROWS = 98304
NB = 768
N_ROW = 16
N_COL = 12
N_SPLIT = 4


def block_pattern(key):
    span = N_SPLIT * (VR // BS)
    row_count = N_COL * span
    col_count = N_ROW * span
    tile_row = jnp.arange(N_ROW, dtype=jnp.int32)[:, None, None]
    tile_col = jnp.arange(N_COL, dtype=jnp.int32)[None, :, None]
    slot_index = jnp.arange(N_SPLIT * MAXB, dtype=jnp.int32)[None, None, :]
    first_slot = (tile_row == 0) & (tile_col == 0) & (slot_index == 0)
    last_col = ((N_ROW - 1) * N_COL + tile_col) * span + span - 1
    row_limit = jnp.clip(last_col - tile_row * row_count, 0, row_count)
    first_key, second_key, third_key = jax.random.split(key, 3)
    slot_shape = (N_ROW, N_COL, N_SPLIT * MAXB)
    local_rows = jax.random.randint(first_key, slot_shape, 0, 1 << 20) % jnp.maximum(row_limit, 1)
    local_rows = jnp.where(first_slot, row_count - 1, local_rows)
    global_rows = tile_row * row_count + local_rows
    col_ids = jnp.arange(col_count, dtype=jnp.int32)
    col_global = (col_ids // span * N_COL + tile_col[..., None]) * span + col_ids % span
    below = jnp.sum((col_global <= global_rows[..., None]).astype(jnp.int32), axis=-1)
    choices_left = col_count - below
    local_cols = below + jax.random.randint(second_key, slot_shape, 0, 1 << 20) % jnp.maximum(choices_left, 1)
    local_cols = jnp.minimum(local_cols, col_count - 1)
    local_cols = jnp.where(first_slot, col_count - 1, local_cols)
    weights_drawn = jax.random.randint(third_key, (N_ROW, N_COL, N_SPLIT), 2, 5)
    split_ids = jnp.arange(N_SPLIT, dtype=jnp.int32)[None, None, :]
    weights_drawn = jnp.where(split_ids == 0, 4, weights_drawn)
    count_limit = jnp.maximum(row_limit, row_count // 2)
    used_counts = (MAXB * count_limit * weights_drawn + 4 * row_count - 1) // (4 * row_count)
    return (local_rows.astype(jnp.int32), local_cols.astype(jnp.int32), used_counts.astype(jnp.int32))


def draw_block_rows(key, part):
    return block_pattern(key)[0]


def draw_block_cols(key, part):
    return block_pattern(key)[1]


def draw_counts(key, part):
    return block_pattern(key)[2]


def draw_start_vectors(key, part):
    key = jax.random.fold_in(key, 7)
    first_key, second_key = jax.random.split(key, 2)
    values = jnp.clip(jax.random.normal(first_key, (NV, ROWS), jnp.float32), -5.0, 5.0)
    scales = jnp.exp(jax.random.uniform(second_key, (1, ROWS), jnp.float32, -1.15, 1.15))
    return values * scales


def draw_diag_energy(key, part):
    key = jax.random.fold_in(key, 11)
    position = jnp.arange(ROWS, dtype=jnp.float32) / ROWS
    factor = jax.random.uniform(key, (ROWS,), jnp.float32, 0.7, 1.3)
    return (1.0 + 2.0 * position) * factor


def block_scale(stream_key, extent, shards, least, top_value):
    def one(dim, blocks):
        steps = jax.random.uniform(jax.random.fold_in(jax.random.fold_in(stream_key, 6), dim), (blocks,), jnp.float32, least / len(shards), top_value / len(shards))
        return jnp.repeat(jnp.exp(steps), extent[dim] // blocks).reshape((-1,) + (1,) * (len(extent) - dim - 1))

    level = one(*shards[0])
    for cut in shards[1:]:
        level = level * one(*cut)
    return level


def scatter_about(own_key, dims, width, limit, cuts=(), kind=jnp.bfloat16):
    result = jax.random.normal(own_key, dims, jnp.float32) * width
    if len(cuts) > 0:
        result = block_scale(own_key, dims, cuts, -0.22, 0.18) * result
    return jnp.clip(result, min=-limit, max=limit).astype(kind)


def setup_inputs(seed: int = 0) -> dict:
    splits = jax.random.split(jax.random.key(seed), 7)
    return {
        "start_vectors": draw_start_vectors(jax.random.fold_in(splits[6], 71), 0),
        "diag_energy": draw_diag_energy(jax.random.fold_in(splits[6], 71), 0),
        "matrix_blocks": scatter_about(splits[2], (N_ROW, N_COL, SLOTS, BS, BS), (MAXB * BS * BS // VR) ** -0.5, 0.125, ((0, 16), (1, 12), (2, 4)), jnp.float32),
        "block_rows": draw_block_rows(jax.random.fold_in(splits[6], 71), 0),
        "block_cols": draw_block_cols(jax.random.fold_in(splits[6], 71), 0),
        "counts": draw_counts(jax.random.fold_in(splits[6], 71), 0),
    }


def apply_hamiltonian(vectors, diag_energy, matrix_blocks, block_rows, block_cols, counts):
    span = N_SPLIT * (VR // BS)
    tiles = N_ROW * N_COL
    blocked = vectors.reshape(NV, NB, BS)
    slot_counts = jnp.repeat(counts, MAXB, axis=2).reshape(tiles, SLOTS)
    tile_blocks = matrix_blocks.reshape(tiles, SLOTS, BS, BS)
    tile_rows = block_rows.reshape(tiles, SLOTS)
    tile_cols = block_cols.reshape(tiles, SLOTS)
    tile_ids = jnp.arange(tiles, dtype=jnp.int32)
    slot_ids = jnp.arange(SLOTS, dtype=jnp.int32) % MAXB

    def add_tile(accumulated, tile_data):
        blocks_here, rows_here, cols_here, count_here, tile_id = tile_data
        row_tile = tile_id // N_COL
        col_tile = tile_id % N_COL
        in_use = (slot_ids < count_here).astype(jnp.float32)
        global_rows = (row_tile * RB + rows_here).astype(jnp.int32)
        global_cols = ((cols_here // span * N_COL + col_tile) * span + cols_here % span).astype(jnp.int32)
        col_inputs = blocked[:, global_cols, :]
        upper_part = jnp.einsum("bij,kbj->kbi", blocks_here, col_inputs, precision=lax.Precision.HIGHEST)
        accumulated = accumulated.at[:, global_rows, :].add(upper_part * in_use[None, :, None])
        row_inputs = blocked[:, global_rows, :]
        lower_part = jnp.einsum("bji,kbj->kbi", blocks_here, row_inputs, precision=lax.Precision.HIGHEST)
        accumulated = accumulated.at[:, global_cols, :].add(lower_part * in_use[None, :, None])
        return accumulated, None

    start = jnp.zeros((NV, NB, BS), jnp.float32)
    accumulated, unused = lax.scan(add_tile, start, (tile_blocks, tile_rows, tile_cols, slot_counts, tile_ids))
    return diag_energy[None, :] * vectors + accumulated.reshape(NV, ROWS)


def reference(start_vectors, diag_energy, matrix_blocks, block_rows, block_cols, counts):
    first_image = apply_hamiltonian(start_vectors, diag_energy, matrix_blocks, block_rows, block_cols, counts)
    correlation = jnp.dot(start_vectors, first_image.T, precision=lax.Precision.HIGHEST) / ROWS
    residual_block = first_image - jnp.dot(correlation.T, start_vectors, precision=lax.Precision.HIGHEST)
    second_image = apply_hamiltonian(residual_block, diag_energy, matrix_blocks, block_rows, block_cols, counts)
    return residual_block, second_image
```

```python
import jax
import jax.numpy as jnp
from jax import lax
from jax.experimental import pallas as pl
from jax.experimental.pallas import tpu as pltpu
from jax.sharding import PartitionSpec as P

HIGHEST = lax.Precision.HIGHEST


def block_products(blocks, row_index, col_index, count, row_in, col_in):
    slots = blocks.shape[0]

    def kernel(row_ids, col_ids, used, u_ref, row_ref, col_ref, row_out, col_out):
        row_out[...] = jnp.zeros_like(row_out)
        col_out[...] = jnp.zeros_like(col_out)
        for t in range(slots):
            keep = jnp.where(t < used[0], 1.0, 0.0).astype(jnp.float32)
            r, c = row_ids[t], col_ids[t]
            u = u_ref[t]
            upper = lax.dot_general(
                col_ref[c], u, (((1,), (1,)), ((), ())), precision=HIGHEST,
                preferred_element_type=jnp.float32,
            )
            lower = lax.dot_general(
                row_ref[r], u, (((1,), (0,)), ((), ())), precision=HIGHEST,
                preferred_element_type=jnp.float32,
            )
            row_out[r] += upper * keep
            col_out[c] += lower * keep

    smem = pl.BlockSpec(memory_space=pltpu.SMEM)
    vmem = pl.BlockSpec(memory_space=pltpu.VMEM)
    return pl.pallas_call(
        kernel,
        out_shape=(
            jax.ShapeDtypeStruct(row_in.shape, jnp.float32),
            jax.ShapeDtypeStruct(col_in.shape, jnp.float32),
        ),
        in_specs=[smem] * 3 + [vmem] * 3,
        out_specs=(vmem, vmem),
        compiler_params=pltpu.CompilerParams(vmem_limit_bytes=16 << 20),
        name="block_products",
    )(row_index, col_index, count, blocks, row_in, col_in)


def share(piece, axis):
    copies = jnp.broadcast_to(piece[None], (lax.axis_size(axis),) + piece.shape)
    return lax.all_to_all(copies, axis, 0, 0, tiled=True)


def exchange(parts, axis):
    return lax.all_to_all(parts, axis, 0, 0, tiled=True)


def on_device(start_vectors, diag_energy, matrix_blocks, block_rows, block_cols, counts):
    rows, cols, splits = (lax.axis_size(a) for a in ("row", "col", "split"))
    vectors, size = start_vectors.shape
    slots = matrix_blocks.shape[2]
    blocks = matrix_blocks.reshape(slots, size, size)
    row_index = block_rows.reshape(slots)
    col_index = block_cols.reshape(slots)
    count = counts.reshape(1)
    total = size * rows * cols * splits
    mine = lax.axis_index("split")
    is_mine = (jnp.arange(splits, dtype=jnp.int32) == mine).astype(jnp.float32)[:, None, None]

    start4 = share(start_vectors, "split")
    row_in = share(start4, "col").reshape(cols * splits, vectors, size)
    col_in = share(start4, "row").reshape(rows * splits, vectors, size)
    row_out, col_out = block_products(blocks, row_index, col_index, count, row_in, col_in)
    row_got = exchange(row_out.reshape(cols, splits, vectors, size), "col")
    col_got = exchange(col_out.reshape(rows, splits, vectors, size), "row")
    part = row_got.sum(0) + col_got.sum(0) + is_mine * (diag_energy[None, :] * start_vectors)[None]
    first4 = share(part, "split").sum(0)
    first = lax.dynamic_index_in_dim(first4, mine, 0, keepdims=False)

    group = jnp.einsum("skg,slg->kl", start4, first4, precision=HIGHEST)
    group = jnp.pad(group, ((0, 0), (0, size - vectors)))
    row_all = share(jnp.concatenate([first4, group[None]], 0), "col")
    tile_corr = row_all[:, splits].sum(0)
    row_in = row_all[:, :splits].reshape(cols * splits, vectors, size)
    col_in = share(first4, "row").reshape(rows * splits, vectors, size)
    row_out, col_out = block_products(blocks, row_index, col_index, count, row_in, col_in)
    row_got = exchange(row_out.reshape(cols, splits, vectors, size), "col")
    col_out = col_out.reshape(rows, splits, vectors, size)
    corr_out = jnp.broadcast_to(tile_corr[None, None], (rows, 1, vectors, size))
    col_got = exchange(jnp.concatenate([col_out, corr_out], 1), "row").sum(0)
    correlation = col_got[splits, :, :vectors] / total
    part = row_got.sum(0) + col_got[:splits]
    image = exchange(part, "split").sum(0) + diag_energy[None, :] * first
    residual = first - jnp.dot(correlation.T, start_vectors, precision=HIGHEST)
    second = image - jnp.dot(correlation.T, first, precision=HIGHEST)
    return residual, second


def solution(mesh):
    in_specs = (
        P(None, ("row", "col", "split")),
        P(("row", "col", "split")),
        P("row", "col", "split", None, None),
        P("row", "col", "split"),
        P("row", "col", "split"),
        P("row", "col", "split"),
    )
    out_specs = (P(None, ("row", "col", "split")), P(None, ("row", "col", "split")))
    return jax.shard_map(
        on_device, mesh=mesh, in_specs=in_specs, out_specs=out_specs, check_vma=False
    )
```

```python
import jax
import jax.numpy as jnp
from jax import lax
from jax.experimental import pallas as pl
from jax.experimental.pallas import tpu as pltpu
from jax.sharding import PartitionSpec as P

HIGHEST = lax.Precision.HIGHEST
SMEM = pl.BlockSpec(memory_space=pltpu.SMEM)
VMEM = pl.BlockSpec(memory_space=pltpu.VMEM)
PARAMS = pltpu.CompilerParams(vmem_limit_bytes=16 << 20)


def arrays(*shapes):
    return tuple(jax.ShapeDtypeStruct(s, jnp.float32) for s in shapes)


def products(ids_from, ids_to, used, u_ref, in_ref, out_ref, block_dim):
    out_ref[...] = jnp.zeros_like(out_ref)
    for t in range(u_ref.shape[0]):
        term = lax.dot_general(
            in_ref[ids_from[t]], u_ref[t], (((1,), (block_dim,)), ((), ())), precision=HIGHEST,
            preferred_element_type=jnp.float32,
        )
        out_ref[ids_to[t]] += term * jnp.where(t < used[0], 1.0, 0.0).astype(jnp.float32)


def block_products(ids_from, ids_to, count, blocks, pieces, out_blocks, block_dim, name):
    slots, size, _ = blocks.shape
    vectors = pieces.shape[1]

    def kernel(a, b, n, u, x, o):
        products(a, b, n, u, x, o, block_dim)

    return pl.pallas_call(
        kernel,
        out_shape=jax.ShapeDtypeStruct((out_blocks, vectors, size), jnp.float32),
        in_specs=[SMEM] * 3 + [VMEM] * 2,
        out_specs=VMEM,
        compiler_params=PARAMS,
        cost_estimate=pl.CostEstimate(
            flops=12 * slots * size * size * vectors, bytes_accessed=4 * slots * size * size,
            transcendentals=0,
        ),
        name=name,
    )(ids_from, ids_to, count, blocks, pieces)


def own_copies(row_piece, place, splits, copies):
    _, vectors, size = row_piece.shape

    def kernel(at, piece, out):
        for s in range(splits):
            block = piece[at[0] * splits + s]
            for i in range(copies):
                out[i, s] = block

    return pl.pallas_call(
        kernel, out_shape=arrays((copies, splits, vectors, size))[0],
        in_specs=[SMEM, VMEM], out_specs=VMEM, compiler_params=PARAMS, name="own_copies",
    )(place, row_piece)


def group_part(row_got, col_got, vectors, diag, place):
    splits = row_got.shape[1]

    def kernel(at, rows, cols, v, d, out):
        own = v[...] * d[...]
        for s in range(splits):
            total = rows[0, s]
            for j in range(1, rows.shape[0]):
                total += rows[j, s]
            for i in range(cols.shape[0]):
                total += cols[i, s]
            total += own * jnp.where(at[0] == s, 1.0, 0.0).astype(jnp.float32)
            for k in range(splits):
                out[k, s] = total

    return pl.pallas_call(
        kernel, out_shape=arrays((splits,) + row_got.shape[1:])[0],
        in_specs=[SMEM] + [VMEM] * 4, out_specs=VMEM, compiler_params=PARAMS, name="group_part",
    )(place, row_got, col_got, vectors, diag)


def image_copies(parts, rows, cols, place):
    splits, _, vectors, size = parts.shape

    def kernel(at, p, col_out, row_out, own):
        for s in range(splits):
            total = p[0, s]
            for k in range(1, splits):
                total += p[k, s]
            for j in range(cols):
                col_out[j, s] = total
            for i in range(rows):
                row_out[i, s] = total
        own[...] = row_out[0, at[0]]

    return pl.pallas_call(
        kernel,
        out_shape=arrays((cols, splits, vectors, size), (rows, splits, vectors, size), (vectors, size)),
        in_specs=[SMEM, VMEM], out_specs=(VMEM,) * 3, compiler_params=PARAMS, name="image_copies",
    )(place, parts)


def products_and_correlation(
    ids_from, ids_to, count, blocks, pieces, start_piece, rows, splits
):
    slots, size, _ = blocks.shape
    tile, vectors, _ = pieces.shape

    def kernel(a, b, n, u, x, v, out):
        out[...] = jnp.zeros_like(out)
        term = jnp.zeros((vectors, vectors), jnp.float32)
        for g in range(tile):
            term += lax.dot_general(
                x[g], v[g], (((1,), (1,)), ((), ())), precision=HIGHEST,
                preferred_element_type=jnp.float32,
            )
        for i in range(rows):
            out[i, splits, :, :vectors] = term
        for t in range(slots):
            product = lax.dot_general(
                x[a[t]], u[t], (((1,), (0,)), ((), ())), precision=HIGHEST,
                preferred_element_type=jnp.float32,
            )
            keep = jnp.where(t < n[0], 1.0, 0.0).astype(jnp.float32)
            to, at = lax.div(b[t], jnp.int32(splits)), lax.rem(b[t], jnp.int32(splits))
            out[to, at] += product * keep

    return pl.pallas_call(
        kernel,
        out_shape=arrays((rows, splits + 1, vectors, size))[0],
        in_specs=[SMEM] * 3 + [VMEM] * 3,
        out_specs=VMEM,
        compiler_params=PARAMS,
        cost_estimate=pl.CostEstimate(
            flops=12 * slots * size * size * vectors, bytes_accessed=4 * slots * size * size,
            transcendentals=0,
        ),
        name="lower_and_correlation",
    )(ids_from, ids_to, count, blocks, pieces, start_piece)


def add_to_messages(col_got, row_out, place):
    rows, more, vectors, size = col_got.shape
    splits = more - 1

    def kernel(at, got, sums, out, corr):
        out[...] = sums[...]
        for s in range(more):
            total = got[0, s]
            for i in range(1, rows):
                total += got[i, s]
            if s < splits:
                out[at[0] * splits + s] += total
            else:
                corr[...] = total

    return pl.pallas_call(
        kernel, out_shape=arrays(row_out.shape, (vectors, size)),
        in_specs=[SMEM, VMEM, VMEM], out_specs=(VMEM, VMEM), compiler_params=PARAMS,
        name="add_to_messages",
    )(place, col_got, row_out)


def subtract(corr, base, value, total):
    scaled = corr[:, : value.shape[0]] * (1.0 / total)
    return base - lax.dot_general(
        scaled, value, (((1,), (0,)), ((), ())), precision=HIGHEST,
        preferred_element_type=jnp.float32,
    )


def residual_of(corr, first, start, total):
    def kernel(c, f, v, out):
        out[...] = subtract(c[...], f[...], v[...], total)

    return pl.pallas_call(
        kernel, out_shape=arrays(first.shape)[0], in_specs=[VMEM] * 3, out_specs=VMEM,
        compiler_params=PARAMS, name="residual",
    )(corr, first, start)


def second_of(got, corr, first, diag, total):
    def kernel(g, c, f, d, out):
        value = f[...]
        image = d[...] * value
        for k in range(g.shape[0]):
            image += g[k]
        out[...] = subtract(c[...], image, value, total)

    return pl.pallas_call(
        kernel, out_shape=arrays(first.shape)[0], in_specs=[VMEM] * 4, out_specs=VMEM,
        compiler_params=PARAMS, name="second",
    )(got, corr, first, diag)


def exchange(parts, axis):
    return lax.all_to_all(parts, axis, 0, 0, tiled=True)


def on_device(start_vectors, diag_energy, matrix_blocks, block_rows, block_cols, counts):
    rows, cols, splits = (lax.axis_size(a) for a in ("row", "col", "split"))
    vectors, size = start_vectors.shape
    slots = matrix_blocks.shape[2]
    blocks = matrix_blocks.reshape(slots, size, size)
    row_ids = block_rows.reshape(slots)
    col_ids = block_cols.reshape(slots)
    count = counts.reshape(1)
    diag = diag_energy.reshape(1, size)
    total = size * rows * cols * splits
    at_col = lax.axis_index("col").astype(jnp.int32).reshape(1)
    at_split = lax.axis_index("split").astype(jnp.int32).reshape(1)
    plane = ("col", "split")

    copies = jnp.broadcast_to(start_vectors[None], (cols * splits, vectors, size))
    start_row = exchange(copies, plane)
    start_col = exchange(own_copies(start_row, at_col, splits, rows), "row")
    lower = block_products(row_ids, col_ids, count, blocks, start_row, rows * splits, 0, "lower")
    col_got = exchange(lower.reshape(rows, splits, vectors, size), "row")
    start_col = start_col.reshape(rows * splits, vectors, size)
    upper = block_products(col_ids, row_ids, count, blocks, start_col, cols * splits, 1, "upper")
    row_got = exchange(upper.reshape(cols, splits, vectors, size), "col")
    parts = exchange(group_part(row_got, col_got, start_vectors, diag, at_split), "split")

    col_copies, row_copies, first = image_copies(parts, rows, cols, at_split)
    first_row = exchange(col_copies, "col").reshape(cols * splits, vectors, size)
    first_col = exchange(row_copies, "row").reshape(rows * splits, vectors, size)
    lower = products_and_correlation(row_ids, col_ids, count, blocks, first_row, start_row, rows, splits)
    col_got = exchange(lower, "row")
    upper = block_products(col_ids, row_ids, count, blocks, first_col, cols * splits, 1, "upper")
    messages, corr = add_to_messages(col_got, upper, at_col)
    got = exchange(messages, plane)
    residual = residual_of(corr, first, start_vectors, total)
    return residual, second_of(got, corr, first, diag, total)


def solution(mesh):
    in_specs = (
        P(None, ("row", "col", "split")),
        P(("row", "col", "split")),
        P("row", "col", "split", None, None),
        P("row", "col", "split"),
        P("row", "col", "split"),
        P("row", "col", "split"),
    )
    out_specs = (P(None, ("row", "col", "split")), P(None, ("row", "col", "split")))
    return jax.shard_map(
        on_device, mesh=mesh, in_specs=in_specs, out_specs=out_specs, check_vma=False
    )
```

```python
import jax
import jax.numpy as jnp
from jax import lax
from jax.experimental import pallas as pl
from jax.experimental.pallas import tpu as pltpu
from jax.sharding import PartitionSpec as P

HIGHEST = lax.Precision.HIGHEST
SMEM = pl.BlockSpec(memory_space=pltpu.SMEM)
VMEM = pl.BlockSpec(memory_space=pltpu.VMEM)
PARAMS = pltpu.CompilerParams(vmem_limit_bytes=16 << 20)


def arrays(*shapes):
    return tuple(jax.ShapeDtypeStruct(s, jnp.float32) for s in shapes)


def add_products(ids_from, ids_to, used, u_ref, in_ref, out_ref, block_dim, from_slot, to_slot):
    for t in range(u_ref.shape[0]):
        term = lax.dot_general(
            in_ref[from_slot(ids_from[t])], u_ref[t], (((1,), (block_dim,)), ((), ())),
            precision=HIGHEST, preferred_element_type=jnp.float32,
        )
        keep = jnp.where(t < used[0], 1.0, 0.0).astype(jnp.float32)
        out_ref[to_slot(ids_to[t])] += term * keep


def same(block):
    return block


def column_slot(splits):
    core = lax.axis_index("core")

    def slot(c):
        row, s = lax.div(c, jnp.int32(splits)), lax.rem(c, jnp.int32(splits))
        y, its_core = lax.div(row, jnp.int32(2)), lax.rem(row, jnp.int32(2))
        other = jnp.where(its_core == core, 0, 1)
        return other, y, s

    return slot


def cost(blocks, vectors):
    return pl.CostEstimate(
        flops=12 * blocks.size * vectors, bytes_accessed=4 * blocks.size, transcendentals=0
    )


def start_copies(start, copies):
    def kernel(v, out):
        block = v[...]
        for i in range(copies):
            out[i] = block

    return pl.pallas_call(
        kernel, out_shape=arrays((copies,) + start.shape)[0], in_specs=[VMEM], out_specs=VMEM,
        compiler_params=PARAMS, name="start_copies",
    )(start)


def upper_products(col_ids, row_ids, count, blocks, own_cols, other_cols, row_blocks):
    ys, splits, vectors, size = own_cols.shape

    def kernel(a, b, n, u, own, other, out, both):
        both[0], both[1] = own[...], other[...]
        out[...] = jnp.zeros_like(out)
        add_products(a, b, n, u, both, out, 1, column_slot(splits), same)

    return pl.pallas_call(
        kernel,
        out_shape=arrays((row_blocks, vectors, size))[0],
        in_specs=[SMEM] * 3 + [VMEM] * 3,
        out_specs=VMEM,
        scratch_shapes=[pltpu.VMEM((2, ys, splits, vectors, size), jnp.float32)],
        compiler_params=PARAMS,
        cost_estimate=cost(blocks, vectors),
        name="upper",
    )(col_ids, row_ids, count, blocks, own_cols, other_cols)


def lower_products(row_ids, col_ids, count, blocks, row_piece, start_piece, ys, splits):
    tile, vectors, size = row_piece.shape
    with_corr = start_piece is not None
    each = splits + 1 if with_corr else splits

    def kernel(a, b, n, u, x, *rest):
        v = rest[0] if with_corr else None
        own, other, both = rest[-3:]
        both[...] = jnp.zeros_like(both)
        if with_corr:
            term = jnp.zeros((vectors, vectors), jnp.float32)
            for g in range(tile):
                term += lax.dot_general(
                    x[g], v[g], (((1,), (1,)), ((), ())), precision=HIGHEST,
                    preferred_element_type=jnp.float32,
                )
            for y in range(ys):
                both[0, y, splits, :, :vectors] = term
                both[1, y, splits, :, :vectors] = term
        add_products(a, b, n, u, x, both, 0, same, column_slot(splits))
        own[...], other[...] = both[0], both[1]

    shape = (ys, each, vectors, size)
    return pl.pallas_call(
        kernel,
        out_shape=arrays(shape, shape),
        in_specs=[SMEM] * 3 + [VMEM] * (3 if with_corr else 2),
        out_specs=(VMEM, VMEM),
        scratch_shapes=[pltpu.VMEM((2,) + shape, jnp.float32)],
        compiler_params=PARAMS,
        cost_estimate=cost(blocks, vectors),
        name="lower",
    )(row_ids, col_ids, count, blocks, row_piece, *((start_piece,) if with_corr else ()))


def add(one, two):
    def kernel(a, b, out):
        out[...] = a[...] + b[...]

    return pl.pallas_call(
        kernel, out_shape=arrays(one.shape)[0], in_specs=[VMEM] * 2, out_specs=VMEM,
        compiler_params=PARAMS, name="add",
    )(one, two)


def own_copies(row_piece, splits, copies):
    _, vectors, size = row_piece.shape

    def kernel(piece, out):
        first = lax.axis_index("col") * splits
        for s in range(splits):
            block = piece[first + s]
            for i in range(copies):
                out[i, s] = block

    return pl.pallas_call(
        kernel, out_shape=arrays((copies, splits, vectors, size))[0],
        in_specs=[VMEM], out_specs=VMEM, compiler_params=PARAMS, name="own_copies",
    )(row_piece)


def group_part(row_got, col_got, vectors, diag):
    splits = row_got.shape[1]

    def kernel(rows, cols, v, d, out):
        own = v[...] * d[...]
        mine = lax.axis_index("split")
        for s in range(splits):
            total = rows[0, s]
            for j in range(1, rows.shape[0]):
                total += rows[j, s]
            for i in range(cols.shape[0]):
                total += cols[i, s]
            total += own * jnp.where(mine == s, 1.0, 0.0).astype(jnp.float32)
            for k in range(splits):
                out[k, s] = total

    return pl.pallas_call(
        kernel, out_shape=arrays((splits,) + row_got.shape[1:])[0],
        in_specs=[VMEM] * 4, out_specs=VMEM, compiler_params=PARAMS, name="group_part",
    )(row_got, col_got, vectors, diag)


def image_copies(parts, ys, cols):
    splits, _, vectors, size = parts.shape

    def kernel(p, col_out, row_out, own):
        for s in range(splits):
            total = p[0, s]
            for k in range(1, splits):
                total += p[k, s]
            for j in range(cols):
                col_out[j, s] = total
            for i in range(ys):
                row_out[i, s] = total
        own[...] = row_out[0, lax.axis_index("split")]

    return pl.pallas_call(
        kernel,
        out_shape=arrays((cols, splits, vectors, size), (ys, splits, vectors, size), (vectors, size)),
        in_specs=[VMEM], out_specs=(VMEM,) * 3, compiler_params=PARAMS, name="image_copies",
    )(parts)


def add_to_messages(col_got, row_out):
    rows, more, vectors, size = col_got.shape
    splits = more - 1

    def kernel(got, sums, out, corr):
        out[...] = sums[...]
        first = lax.axis_index("col") * splits
        for s in range(more):
            total = got[0, s]
            for i in range(1, rows):
                total += got[i, s]
            if s < splits:
                out[first + s] += total
            else:
                corr[...] = total

    return pl.pallas_call(
        kernel, out_shape=arrays(row_out.shape, (vectors, size)),
        in_specs=[VMEM, VMEM], out_specs=(VMEM, VMEM), compiler_params=PARAMS,
        name="add_to_messages",
    )(col_got, row_out)


def subtract(corr, base, value, total):
    scaled = corr[:, : value.shape[0]] * (1.0 / total)
    return base - lax.dot_general(
        scaled, value, (((1,), (0,)), ((), ())), precision=HIGHEST,
        preferred_element_type=jnp.float32,
    )


def residual_of(corr, first, start, total):
    def kernel(c, f, v, out):
        out[...] = subtract(c[...], f[...], v[...], total)

    return pl.pallas_call(
        kernel, out_shape=arrays(first.shape)[0], in_specs=[VMEM] * 3, out_specs=VMEM,
        compiler_params=PARAMS, name="residual",
    )(corr, first, start)


def second_of(got, corr, first, diag, total):
    def kernel(g, c, f, d, out):
        value = f[...]
        image = d[...] * value
        for k in range(g.shape[0]):
            image += g[k]
        out[...] = subtract(c[...], image, value, total)

    return pl.pallas_call(
        kernel, out_shape=arrays(first.shape)[0], in_specs=[VMEM] * 4, out_specs=VMEM,
        compiler_params=PARAMS, name="second",
    )(got, corr, first, diag)


def exchange(parts, axis):
    return lax.all_to_all(parts, axis, 0, 0, tiled=True)


def swap_cores(piece):
    return lax.ppermute(piece, "core", [(0, 1), (1, 0)])


def on_device(start_vectors, diag_energy, matrix_blocks, block_rows, block_cols, counts):
    ys, cols, splits = (lax.axis_size(a) for a in ("y", "col", "split"))
    vectors, size = start_vectors.shape
    slots = matrix_blocks.shape[2]
    blocks = matrix_blocks.reshape(slots, size, size)
    row_ids = block_rows.reshape(slots)
    col_ids = block_cols.reshape(slots)
    count = counts.reshape(1)
    diag = diag_energy.reshape(1, size)
    total = size * ys * 2 * cols * splits
    plane = ("col", "split")

    start_row = exchange(start_copies(start_vectors, cols * splits), plane)
    own_cols = exchange(own_copies(start_row, splits, ys), "y")
    own, other = lower_products(row_ids, col_ids, count, blocks, start_row, None, ys, splits)
    col_got = exchange(add(own, swap_cores(other)), "y")
    upper = upper_products(
        col_ids, row_ids, count, blocks, own_cols, swap_cores(own_cols), cols * splits
    )
    row_got = exchange(upper.reshape(cols, splits, vectors, size), "col")
    parts = exchange(group_part(row_got, col_got, start_vectors, diag), "split")

    col_copies, y_copies, first = image_copies(parts, ys, cols)
    first_row = exchange(col_copies, "col").reshape(cols * splits, vectors, size)
    own_cols = exchange(y_copies, "y")
    own, other = lower_products(row_ids, col_ids, count, blocks, first_row, start_row, ys, splits)
    col_got = exchange(add(own, swap_cores(other)), "y")
    upper = upper_products(
        col_ids, row_ids, count, blocks, own_cols, swap_cores(own_cols), cols * splits
    )
    messages, corr = add_to_messages(col_got, upper)
    got = exchange(messages, plane)
    residual = residual_of(corr, first, start_vectors, total)
    return residual, second_of(got, corr, first, diag, total)


def solution(mesh):
    rows, cols, splits = mesh.devices.shape
    axes = ("y", "core", "col", "split")
    mesh = jax.sharding.Mesh(mesh.devices.reshape(rows // 2, 2, cols, splits), axes)
    row = ("y", "core")
    in_specs = (
        P(None, axes),
        P(axes),
        P(row, "col", "split", None, None),
        P(row, "col", "split"),
        P(row, "col", "split"),
        P(row, "col", "split"),
    )
    out_specs = (P(None, axes), P(None, axes))
    return jax.shard_map(
        on_device, mesh=mesh, in_specs=in_specs, out_specs=out_specs, check_vma=False
    )
```

```python
import jax
import jax.numpy as jnp
from jax import lax
from jax.experimental import pallas as pl
from jax.experimental.pallas import tpu as pltpu
from jax.sharding import PartitionSpec as P

HIGHEST = lax.Precision.HIGHEST
SMEM = pl.BlockSpec(memory_space=pltpu.SMEM)
VMEM = pl.BlockSpec(memory_space=pltpu.VMEM)
PARAMS = pltpu.CompilerParams(vmem_limit_bytes=16 << 20)


def arrays(*shapes):
    return tuple(jax.ShapeDtypeStruct(s, jnp.float32) for s in shapes)


def add_products(ids_from, ids_to, used, u_ref, in_ref, out_ref, block_dim, from_slot, to_slot):
    for t in range(u_ref.shape[0]):
        term = lax.dot_general(
            in_ref[from_slot(ids_from[t])], u_ref[t], (((1,), (block_dim,)), ((), ())),
            precision=HIGHEST, preferred_element_type=jnp.float32,
        )
        keep = jnp.where(t < used[0], 1.0, 0.0).astype(jnp.float32)
        out_ref[to_slot(ids_to[t])] += term * keep


def same(block):
    return block


def column_slot(splits):
    core = lax.axis_index("core")

    def slot(c):
        row, s = lax.div(c, jnp.int32(splits)), lax.rem(c, jnp.int32(splits))
        y, its_core = lax.div(row, jnp.int32(2)), lax.rem(row, jnp.int32(2))
        return y, jnp.where(its_core == core, 0, splits) + s

    return slot


def cost(blocks, vectors):
    return pl.CostEstimate(
        flops=12 * blocks.size * vectors, bytes_accessed=4 * blocks.size, transcendentals=0
    )


def start_copies(start, copies):
    def kernel(v, out):
        block = v[...]
        for i in range(copies):
            out[i] = block

    return pl.pallas_call(
        kernel, out_shape=arrays((copies,) + start.shape)[0], in_specs=[VMEM], out_specs=VMEM,
        compiler_params=PARAMS, name="start_copies",
    )(start)


def upper_products(col_ids, row_ids, count, blocks, col_pieces, row_blocks, splits):
    ys, _, vectors, size = col_pieces[0].shape
    parts = len(col_pieces)
    each = 2 * splits // parts

    def kernel(a, b, n, u, *rest):
        pieces, out = rest[:parts], rest[parts]
        both = pieces[0]
        if parts > 1:
            both = rest[-1]
            for k in range(parts):
                both[:, k * each : (k + 1) * each] = pieces[k][...]
        out[...] = jnp.zeros_like(out)
        add_products(a, b, n, u, both, out, 1, column_slot(splits), same)

    scratch = pltpu.VMEM((ys, 2 * splits, vectors, size), jnp.float32)
    return pl.pallas_call(
        kernel,
        out_shape=arrays((row_blocks, vectors, size))[0],
        in_specs=[SMEM] * 3 + [VMEM] * (1 + parts),
        out_specs=VMEM,
        scratch_shapes=[scratch] if parts > 1 else [],
        compiler_params=PARAMS,
        cost_estimate=cost(blocks, vectors),
        name="upper",
    )(col_ids, row_ids, count, blocks, *col_pieces)


def lower_products(row_ids, col_ids, count, blocks, row_piece, ys, splits):
    _, vectors, size = row_piece.shape

    def kernel(a, b, n, u, x, out):
        out[...] = jnp.zeros_like(out)
        add_products(a, b, n, u, x, out, 0, same, column_slot(splits))

    return pl.pallas_call(
        kernel,
        out_shape=arrays((ys, 2 * splits, vectors, size))[0],
        in_specs=[SMEM] * 3 + [VMEM] * 2,
        out_specs=VMEM,
        compiler_params=PARAMS,
        cost_estimate=cost(blocks, vectors),
        name="lower",
    )(row_ids, col_ids, count, blocks, row_piece)


def lower_and_correlation(row_ids, col_ids, count, blocks, row_piece, start_piece, ys, splits):
    tile, vectors, size = row_piece.shape

    def kernel(a, b, n, u, x, v, own, other, both):
        both[...] = jnp.zeros_like(both)
        add_products(a, b, n, u, x, both, 0, same, column_slot(splits))
        term = jnp.zeros((vectors, vectors), jnp.float32)
        for g in range(tile):
            term += lax.dot_general(
                x[g], v[g], (((1,), (1,)), ((), ())), precision=HIGHEST,
                preferred_element_type=jnp.float32,
            )
        for k, out in enumerate((own, other)):
            out[:, :splits] = both[:, k * splits : (k + 1) * splits]
            out[:, splits] = jnp.zeros((ys, vectors, size), jnp.float32)
            for y in range(ys):
                out[y, splits, :, :vectors] = term

    shape = (ys, splits + 1, vectors, size)
    return pl.pallas_call(
        kernel,
        out_shape=arrays(shape, shape),
        in_specs=[SMEM] * 3 + [VMEM] * 3,
        out_specs=(VMEM, VMEM),
        scratch_shapes=[pltpu.VMEM((ys, 2 * splits, vectors, size), jnp.float32)],
        compiler_params=PARAMS,
        cost_estimate=cost(blocks, vectors),
        name="lower_and_correlation",
    )(row_ids, col_ids, count, blocks, row_piece, start_piece)


def column_sums(col_got, splits):
    ys, _, vectors, size = col_got.shape

    def kernel(got, own, other):
        for k, out in enumerate((own, other)):
            for s in range(splits):
                total = got[0, k * splits + s]
                for y in range(1, ys):
                    total += got[y, k * splits + s]
                out[s] = total

    shape = (splits, vectors, size)
    return pl.pallas_call(
        kernel, out_shape=arrays(shape, shape), in_specs=[VMEM], out_specs=(VMEM, VMEM),
        compiler_params=PARAMS, name="column_sums",
    )(col_got)


def add(one, two):
    def kernel(a, b, out):
        out[...] = a[...] + b[...]

    return pl.pallas_call(
        kernel, out_shape=arrays(one.shape)[0], in_specs=[VMEM] * 2, out_specs=VMEM,
        compiler_params=PARAMS, name="add",
    )(one, two)


def own_copies(row_piece, diag, splits, copies):
    _, vectors, size = row_piece.shape

    def kernel(piece, d, out, scaled):
        first = lax.axis_index("col") * splits
        for s in range(splits):
            block = piece[first + s]
            for i in range(copies):
                out[i, s] = block
        scaled[...] = piece[first + lax.axis_index("split")] * d[...]

    return pl.pallas_call(
        kernel, out_shape=arrays((copies, splits, vectors, size), (vectors, size)),
        in_specs=[VMEM] * 2, out_specs=(VMEM,) * 2, compiler_params=PARAMS, name="own_copies",
    )(row_piece, diag)


def group_part(row_got, own_sum, other_sum, scaled):
    splits = row_got.shape[1]

    def kernel(rows, one, two, own, out):
        mine = lax.axis_index("split")
        for s in range(splits):
            total = one[s] + two[s]
            for j in range(rows.shape[0]):
                total += rows[j, s]
            total += own[...] * jnp.where(mine == s, 1.0, 0.0).astype(jnp.float32)
            for k in range(splits):
                out[k, s] = total

    return pl.pallas_call(
        kernel, out_shape=arrays((splits,) + row_got.shape[1:])[0],
        in_specs=[VMEM] * 4, out_specs=VMEM, compiler_params=PARAMS, name="group_part",
    )(row_got, own_sum, other_sum, scaled)


def image_copies(parts, cols):
    splits, _, vectors, size = parts.shape

    def kernel(p, col_out, image, own):
        for s in range(splits):
            total = p[0, s]
            for k in range(1, splits):
                total += p[k, s]
            image[s] = total
            for j in range(cols):
                col_out[j, s] = total
        own[...] = image[lax.axis_index("split")]

    group = (splits, vectors, size)
    return pl.pallas_call(
        kernel, out_shape=arrays((cols,) + group, group, (vectors, size)),
        in_specs=[VMEM], out_specs=(VMEM,) * 3, compiler_params=PARAMS, name="image_copies",
    )(parts)


def y_copies(own, other, ys):
    splits, vectors, size = own.shape

    def kernel(one, two, out):
        for y in range(ys):
            out[y, :splits] = one[...]
            out[y, splits:] = two[...]

    return pl.pallas_call(
        kernel, out_shape=arrays((ys, 2 * splits, vectors, size))[0], in_specs=[VMEM] * 2,
        out_specs=VMEM, compiler_params=PARAMS, name="y_copies",
    )(own, other)


def add_to_messages(col_got, row_out):
    rows, more, vectors, size = col_got.shape
    splits = more - 1

    def kernel(got, sums, out, corr):
        out[...] = sums[...]
        first = lax.axis_index("col") * splits
        for s in range(more):
            total = got[0, s]
            for i in range(1, rows):
                total += got[i, s]
            if s < splits:
                out[first + s] += total
            else:
                corr[...] = total

    return pl.pallas_call(
        kernel, out_shape=arrays(row_out.shape, (vectors, size)),
        in_specs=[VMEM, VMEM], out_specs=(VMEM, VMEM), compiler_params=PARAMS,
        name="add_to_messages",
    )(col_got, row_out)


def subtract(corr, base, value, total):
    scaled = corr[:, : value.shape[0]] * (1.0 / total)
    return base - lax.dot_general(
        scaled, value, (((1,), (0,)), ((), ())), precision=HIGHEST,
        preferred_element_type=jnp.float32,
    )


def results(got, corr, first, start, diag, total):
    def kernel(g, c, f, v, d, residual, second):
        value = f[...]
        image = d[...] * value
        for k in range(g.shape[0]):
            image += g[k]
        residual[...] = subtract(c[...], value, v[...], total)
        second[...] = subtract(c[...], image, value, total)

    return pl.pallas_call(
        kernel, out_shape=arrays(first.shape, first.shape), in_specs=[VMEM] * 5,
        out_specs=(VMEM, VMEM), compiler_params=PARAMS, name="results",
    )(got, corr, first, start, diag)


def exchange(parts, axis):
    return lax.all_to_all(parts, axis, 0, 0, tiled=True)


def swap_cores(piece):
    return lax.ppermute(piece, "core", [(0, 1), (1, 0)])


def on_device(start_vectors, diag_energy, matrix_blocks, block_rows, block_cols, counts):
    ys, cols, splits = (lax.axis_size(a) for a in ("y", "col", "split"))
    vectors, size = start_vectors.shape
    slots = matrix_blocks.shape[2]
    blocks = matrix_blocks.reshape(slots, size, size)
    row_ids = block_rows.reshape(slots)
    col_ids = block_cols.reshape(slots)
    count = counts.reshape(1)
    diag = diag_energy.reshape(1, size)
    total = size * ys * 2 * cols * splits
    plane = ("col", "split")

    start_row = exchange(start_copies(start_vectors, cols * splits), plane)
    copies, scaled = own_copies(start_row, diag, splits, ys)
    own_cols = exchange(copies, "y")
    lower = lower_products(row_ids, col_ids, count, blocks, start_row, ys, splits)
    col_got = exchange(lower, "y")
    upper = upper_products(
        col_ids, row_ids, count, blocks, (own_cols, swap_cores(own_cols)), cols * splits, splits
    )
    row_got = exchange(upper.reshape(cols, splits, vectors, size), "col")
    own_sum, other_sum = column_sums(col_got, splits)
    parts = exchange(group_part(row_got, own_sum, swap_cores(other_sum), scaled), "split")

    col_copies, image, first = image_copies(parts, cols)
    first_row = exchange(col_copies, "col").reshape(cols * splits, vectors, size)
    both_cols = exchange(y_copies(image, swap_cores(image), ys), "y")
    own, other = lower_and_correlation(
        row_ids, col_ids, count, blocks, first_row, start_row, ys, splits
    )
    col_got = exchange(add(own, swap_cores(other)), "y")
    upper = upper_products(col_ids, row_ids, count, blocks, (both_cols,), cols * splits, splits)
    messages, corr = add_to_messages(col_got, upper)
    got = exchange(messages, plane)
    return results(got, corr, first, start_vectors, diag, total)


def solution(mesh):
    rows, cols, splits = mesh.devices.shape
    axes = ("y", "core", "col", "split")
    mesh = jax.sharding.Mesh(mesh.devices.reshape(rows // 2, 2, cols, splits), axes)
    row = ("y", "core")
    in_specs = (
        P(None, axes),
        P(axes),
        P(row, "col", "split", None, None),
        P(row, "col", "split"),
        P(row, "col", "split"),
        P(row, "col", "split"),
    )
    out_specs = (P(None, axes), P(None, axes))
    return jax.shard_map(
        on_device, mesh=mesh, in_specs=in_specs, out_specs=out_specs, check_vma=False
    )
```

```python
import jax
import jax.numpy as jnp
from jax import lax
from jax.experimental import pallas as pl
from jax.experimental.pallas import tpu as pltpu
from jax.sharding import PartitionSpec as P

HIGHEST = lax.Precision.HIGHEST
SMEM = pl.BlockSpec(memory_space=pltpu.SMEM)
VMEM = pl.BlockSpec(memory_space=pltpu.VMEM)
PARAMS = pltpu.CompilerParams(vmem_limit_bytes=16 << 20)


def arrays(*shapes):
    return tuple(jax.ShapeDtypeStruct(s, jnp.float32) for s in shapes)


def halves(x):
    high = x.astype(jnp.bfloat16)
    return high, (x - high.astype(jnp.float32)).astype(jnp.bfloat16)


def prepare(row_ids, col_ids, count, blocks, start, diag, splits):
    slots, size, _ = blocks.shape

    def kernel(r, c, n, u, v, d, lower, upper, table, scaled):
        core = lax.axis_index("core")
        for t in range(slots):
            row, split = lax.div(c[t], jnp.int32(splits)), lax.rem(c[t], jnp.int32(splits))
            table[t] = r[t]
            table[slots + t] = jnp.where(lax.rem(row, jnp.int32(2)) == core, 0, 1)
            table[2 * slots + t] = lax.div(row, jnp.int32(2))
            table[3 * slots + t] = split
            block = u[t] * jnp.where(t < n[0], 1.0, 0.0).astype(jnp.float32)
            for out, x in ((lower, block), (upper, block.T)):
                high, low = halves(x)
                out[t, :, :size] = high
                out[t, :, size:] = low
        scaled[...] = v[...] * d[...]

    both = jax.ShapeDtypeStruct((slots, size, 2 * size), jnp.bfloat16)
    return pl.pallas_call(
        kernel,
        out_shape=(
            both, both, jax.ShapeDtypeStruct((4 * slots,), jnp.int32),
            jax.ShapeDtypeStruct(start.shape, jnp.float32),
        ),
        in_specs=[SMEM] * 3 + [VMEM] * 3,
        out_specs=(VMEM, VMEM, SMEM, VMEM),
        compiler_params=PARAMS,
        cost_estimate=pl.CostEstimate(
            flops=8 * blocks.size, bytes_accessed=12 * blocks.size, transcendentals=0
        ),
        name="prepare",
    )(row_ids, col_ids, count, blocks, start, diag)


def product(x, block):
    rows, size = x.shape
    high = x.astype(jnp.bfloat16).astype(jnp.float32)
    pair = jnp.concatenate([high, x - high], 0).astype(jnp.bfloat16)
    terms = lax.dot_general(
        pair, block, (((1,), (0,)), ((), ())), preferred_element_type=jnp.float32
    )
    terms = terms[:rows] + terms[rows:]
    return terms[:, :size] + terms[:, size:]


def pair_sums(one, two):
    blocks, vectors, size = one.shape
    sums = [jnp.zeros((vectors, size), jnp.float32) for _ in range(vectors)]
    for g in range(blocks):
        x, v = one[g], two[g]
        for r in range(vectors):
            sums[r] += x * (pltpu.roll(v, r, 0) if r else v)
    l = lax.broadcasted_iota(jnp.int32, (vectors, vectors), 0)
    k = lax.broadcasted_iota(jnp.int32, (vectors, vectors), 1)
    out = jnp.zeros((vectors, vectors), jnp.float32)
    for r in range(vectors):
        its = (l - k == r) | (l - k == r - vectors)
        out += jnp.where(its, jnp.sum(sums[r], axis=1, keepdims=True), 0.0)
    return out


def cost(blocks, vectors):
    return pl.CostEstimate(
        flops=4 * blocks.size * vectors, bytes_accessed=2 * blocks.size, transcendentals=0
    )


def start_copies(start, copies):
    def kernel(v, out):
        block = v[...]
        for i in range(copies):
            out[i] = block

    return pl.pallas_call(
        kernel, out_shape=arrays((copies,) + start.shape)[0], in_specs=[VMEM], out_specs=VMEM,
        compiler_params=PARAMS, name="start_copies",
    )(start)


def upper_products(table, blocks, own_cols, other_cols, row_blocks):
    ys, splits, vectors, size = own_cols.shape
    slots = blocks.shape[0]

    def kernel(at, u, own, other, out, both):
        both[0], both[1] = own[...], other[...]
        out[...] = jnp.zeros_like(out)
        for t in range(slots):
            x = both[at[slots + t], at[2 * slots + t], at[3 * slots + t]]
            out[at[t]] += product(x, u[t])

    return pl.pallas_call(
        kernel,
        out_shape=arrays((row_blocks, vectors, size))[0],
        in_specs=[SMEM] + [VMEM] * 3,
        out_specs=VMEM,
        scratch_shapes=[pltpu.VMEM((2, ys, splits, vectors, size), jnp.float32)],
        compiler_params=PARAMS,
        cost_estimate=cost(blocks, vectors),
        name="upper",
    )(table, blocks, own_cols, other_cols)


def lower_products(table, blocks, row_piece, start_piece, ys, splits):
    _, vectors, size = row_piece.shape
    slots = blocks.shape[0]
    with_corr = start_piece is not None
    each = splits + 1 if with_corr else splits

    def kernel(at, u, x, *rest):
        own, other, both = rest[-3:]
        both[...] = jnp.zeros_like(both)
        for t in range(slots):
            place = at[slots + t], at[2 * slots + t], at[3 * slots + t]
            both[place] += product(x[at[t]], u[t])
        if with_corr:
            term = pair_sums(x, rest[0])
            for y in range(ys):
                both[0, y, splits, :, :vectors] = term
                both[1, y, splits, :, :vectors] = term
        own[...], other[...] = both[0], both[1]

    shape = (ys, each, vectors, size)
    return pl.pallas_call(
        kernel,
        out_shape=arrays(shape, shape),
        in_specs=[SMEM] + [VMEM] * (3 if with_corr else 2),
        out_specs=(VMEM, VMEM),
        scratch_shapes=[pltpu.VMEM((2,) + shape, jnp.float32)],
        compiler_params=PARAMS,
        cost_estimate=cost(blocks, vectors),
        name="lower",
    )(table, blocks, row_piece, *((start_piece,) if with_corr else ()))


def add(one, two):
    def kernel(a, b, out):
        out[...] = a[...] + b[...]

    return pl.pallas_call(
        kernel, out_shape=arrays(one.shape)[0], in_specs=[VMEM] * 2, out_specs=VMEM,
        compiler_params=PARAMS, name="add",
    )(one, two)


def own_copies(row_piece, prepared, splits, copies):
    _, vectors, size = row_piece.shape

    def kernel(piece, _, out):
        first = lax.axis_index("col") * splits
        for s in range(splits):
            block = piece[first + s]
            for i in range(copies):
                out[i, s] = block

    return pl.pallas_call(
        kernel, out_shape=arrays((copies, splits, vectors, size))[0],
        in_specs=[VMEM] * 2, out_specs=VMEM, compiler_params=PARAMS, name="own_copies",
    )(row_piece, prepared)


def group_part(row_got, col_got, scaled):
    splits = row_got.shape[1]

    def kernel(rows, cols, own, out):
        mine = lax.axis_index("split")
        for s in range(splits):
            total = rows[0, s]
            for j in range(1, rows.shape[0]):
                total += rows[j, s]
            for i in range(cols.shape[0]):
                total += cols[i, s]
            total += own[...] * jnp.where(mine == s, 1.0, 0.0).astype(jnp.float32)
            for k in range(splits):
                out[k, s] = total

    return pl.pallas_call(
        kernel, out_shape=arrays((splits,) + row_got.shape[1:])[0],
        in_specs=[VMEM] * 3, out_specs=VMEM, compiler_params=PARAMS, name="group_part",
    )(row_got, col_got, scaled)


def image_copies(parts, ys, cols):
    splits, _, vectors, size = parts.shape

    def kernel(p, col_out, row_out, own):
        for s in range(splits):
            total = p[0, s]
            for k in range(1, splits):
                total += p[k, s]
            for j in range(cols):
                col_out[j, s] = total
            for i in range(ys):
                row_out[i, s] = total
        own[...] = row_out[0, lax.axis_index("split")]

    return pl.pallas_call(
        kernel,
        out_shape=arrays((cols, splits, vectors, size), (ys, splits, vectors, size), (vectors, size)),
        in_specs=[VMEM], out_specs=(VMEM,) * 3, compiler_params=PARAMS, name="image_copies",
    )(parts)


def add_to_messages(col_got, row_out):
    rows, more, vectors, size = col_got.shape
    splits = more - 1

    def kernel(got, sums, out, corr):
        out[...] = sums[...]
        first = lax.axis_index("col") * splits
        for s in range(more):
            total = got[0, s]
            for i in range(1, rows):
                total += got[i, s]
            if s < splits:
                out[first + s] += total
            else:
                corr[...] = total

    return pl.pallas_call(
        kernel, out_shape=arrays(row_out.shape, (vectors, size)),
        in_specs=[VMEM, VMEM], out_specs=(VMEM, VMEM), compiler_params=PARAMS,
        name="add_to_messages",
    )(col_got, row_out)


def subtract(corr, base, value, total):
    scaled = corr[:, : value.shape[0]] * (1.0 / total)
    return base - lax.dot_general(
        scaled, value, (((1,), (0,)), ((), ())), precision=HIGHEST,
        preferred_element_type=jnp.float32,
    )


def residual_of(corr, first, start, total):
    def kernel(c, f, v, out):
        out[...] = subtract(c[...], f[...], v[...], total)

    return pl.pallas_call(
        kernel, out_shape=arrays(first.shape)[0], in_specs=[VMEM] * 3, out_specs=VMEM,
        compiler_params=PARAMS, name="residual",
    )(corr, first, start)


def second_of(got, corr, first, diag, total):
    def kernel(g, c, f, d, out):
        value = f[...]
        image = d[...] * value
        for k in range(g.shape[0]):
            image += g[k]
        out[...] = subtract(c[...], image, value, total)

    return pl.pallas_call(
        kernel, out_shape=arrays(first.shape)[0], in_specs=[VMEM] * 4, out_specs=VMEM,
        compiler_params=PARAMS, name="second",
    )(got, corr, first, diag)


def exchange(parts, axis):
    return lax.all_to_all(parts, axis, 0, 0, tiled=True)


def swap_cores(piece):
    return lax.ppermute(piece, "core", [(0, 1), (1, 0)])


def on_device(start_vectors, diag_energy, matrix_blocks, block_rows, block_cols, counts):
    ys, cols, splits = (lax.axis_size(a) for a in ("y", "col", "split"))
    vectors, size = start_vectors.shape
    slots = matrix_blocks.shape[2]
    blocks = matrix_blocks.reshape(slots, size, size)
    row_ids = block_rows.reshape(slots)
    col_ids = block_cols.reshape(slots)
    count = counts.reshape(1)
    diag = diag_energy.reshape(1, size)
    total = size * ys * 2 * cols * splits
    plane = ("col", "split")

    start_row = exchange(start_copies(start_vectors, cols * splits), plane)
    lower, upper, table, scaled = prepare(
        row_ids, col_ids, count, blocks, start_vectors, diag, splits
    )
    own_cols = exchange(own_copies(start_row, scaled, splits, ys), "y")
    own, other = lower_products(table, lower, start_row, None, ys, splits)
    col_got = exchange(add(own, swap_cores(other)), "y")
    rows = upper_products(table, upper, own_cols, swap_cores(own_cols), cols * splits)
    row_got = exchange(rows.reshape(cols, splits, vectors, size), "col")
    parts = exchange(group_part(row_got, col_got, scaled), "split")

    col_copies, y_copies, first = image_copies(parts, ys, cols)
    first_row = exchange(col_copies, "col").reshape(cols * splits, vectors, size)
    own_cols = exchange(y_copies, "y")
    own, other = lower_products(table, lower, first_row, start_row, ys, splits)
    col_got = exchange(add(own, swap_cores(other)), "y")
    rows = upper_products(table, upper, own_cols, swap_cores(own_cols), cols * splits)
    messages, corr = add_to_messages(col_got, rows)
    got = exchange(messages, plane)
    residual = residual_of(corr, first, start_vectors, total)
    return residual, second_of(got, corr, first, diag, total)


def solution(mesh):
    rows, cols, splits = mesh.devices.shape
    axes = ("y", "core", "col", "split")
    mesh = jax.sharding.Mesh(mesh.devices.reshape(rows // 2, 2, cols, splits), axes)
    row = ("y", "core")
    in_specs = (
        P(None, axes),
        P(axes),
        P(row, "col", "split", None, None),
        P(row, "col", "split"),
        P(row, "col", "split"),
        P(row, "col", "split"),
    )
    out_specs = (P(None, axes), P(None, axes))
    return jax.shard_map(
        on_device, mesh=mesh, in_specs=in_specs, out_specs=out_specs, check_vma=False
    )
```

```python
import jax
import jax.numpy as jnp
from jax import lax
from jax.experimental import pallas as pl
from jax.experimental.pallas import tpu as pltpu
from jax.sharding import PartitionSpec as P

HIGHEST = lax.Precision.HIGHEST
SMEM = pl.BlockSpec(memory_space=pltpu.SMEM)
VMEM = pl.BlockSpec(memory_space=pltpu.VMEM)
PARAMS = pltpu.CompilerParams(vmem_limit_bytes=16 << 20)


def arrays(*shapes):
    return tuple(jax.ShapeDtypeStruct(s, jnp.float32) for s in shapes)


def halves(x):
    high = x.astype(jnp.bfloat16)
    return high, (x - high.astype(jnp.float32)).astype(jnp.bfloat16)


def prepare(row_ids, col_ids, count, blocks, start, diag, splits):
    slots, size, _ = blocks.shape

    def kernel(r, c, n, u, v, d, lower, upper, table, scaled):
        core = lax.axis_index("core")
        for t in range(slots):
            row, split = lax.div(c[t], jnp.int32(splits)), lax.rem(c[t], jnp.int32(splits))
            table[t] = r[t]
            table[slots + t] = jnp.where(lax.rem(row, jnp.int32(2)) == core, 0, 1)
            table[2 * slots + t] = lax.div(row, jnp.int32(2))
            table[3 * slots + t] = split
            table[4 * slots + t] = lax.rem(row, jnp.int32(2))
            block = u[t] * jnp.where(t < n[0], 1.0, 0.0).astype(jnp.float32)
            for out, x in ((lower, block), (upper, block.T)):
                high, low = halves(x)
                out[t, :, :size] = high
                out[t, :, size:] = low
        scaled[...] = v[...] * d[...]

    both = jax.ShapeDtypeStruct((slots, size, 2 * size), jnp.bfloat16)
    return pl.pallas_call(
        kernel,
        out_shape=(
            both, both, jax.ShapeDtypeStruct((5 * slots,), jnp.int32),
            jax.ShapeDtypeStruct(start.shape, jnp.float32),
        ),
        in_specs=[SMEM] * 3 + [VMEM] * 3,
        out_specs=(VMEM, VMEM, SMEM, VMEM),
        compiler_params=PARAMS,
        cost_estimate=pl.CostEstimate(
            flops=8 * blocks.size, bytes_accessed=12 * blocks.size, transcendentals=0
        ),
        name="prepare",
    )(row_ids, col_ids, count, blocks, start, diag)


def product(x, block):
    rows, size = x.shape
    high = x.astype(jnp.bfloat16).astype(jnp.float32)
    pair = jnp.concatenate([high, x - high], 0).astype(jnp.bfloat16)
    terms = lax.dot_general(
        pair, block, (((1,), (0,)), ((), ())), preferred_element_type=jnp.float32
    )
    terms = terms[:rows] + terms[rows:]
    return terms[:, :size] + terms[:, size:]


def pair_sums(one, two):
    blocks, vectors, size = one.shape
    sums = [jnp.zeros((vectors, size), jnp.float32) for _ in range(vectors)]
    for g in range(blocks):
        x, v = one[g], two[g]
        for r in range(vectors):
            sums[r] += x * (pltpu.roll(v, r, 0) if r else v)
    l = lax.broadcasted_iota(jnp.int32, (vectors, vectors), 0)
    k = lax.broadcasted_iota(jnp.int32, (vectors, vectors), 1)
    out = jnp.zeros((vectors, vectors), jnp.float32)
    for r in range(vectors):
        its = (l - k == r) | (l - k == r - vectors)
        out += jnp.where(its, jnp.sum(sums[r], axis=1, keepdims=True), 0.0)
    return out


def cost(blocks, vectors):
    return pl.CostEstimate(
        flops=4 * blocks.size * vectors, bytes_accessed=2 * blocks.size, transcendentals=0
    )


def start_copies(start, copies):
    def kernel(v, out):
        block = v[...]
        for i in range(copies):
            out[i] = block

    return pl.pallas_call(
        kernel, out_shape=arrays((copies,) + start.shape)[0], in_specs=[VMEM], out_specs=VMEM,
        compiler_params=PARAMS, name="start_copies",
    )(start)


def upper_products(table, blocks, cols, row_blocks):
    _, _, _, vectors, size = cols.shape
    slots = blocks.shape[0]

    def kernel(at, u, x, out):
        out[...] = jnp.zeros_like(out)
        for t in range(slots):
            place = at[4 * slots + t], at[2 * slots + t], at[3 * slots + t]
            out[at[t]] += product(x[place], u[t])

    return pl.pallas_call(
        kernel,
        out_shape=arrays((row_blocks, vectors, size))[0],
        in_specs=[SMEM] + [VMEM] * 2,
        out_specs=VMEM,
        compiler_params=PARAMS,
        cost_estimate=cost(blocks, vectors),
        name="upper",
    )(table, blocks, cols)


def lower_products(table, blocks, row_piece, start_piece, ys, splits):
    _, vectors, size = row_piece.shape
    slots = blocks.shape[0]
    with_corr = start_piece is not None
    each = splits + 1 if with_corr else splits

    def kernel(at, u, x, *rest):
        own, other, both = rest[-3:]
        both[...] = jnp.zeros_like(both)
        for t in range(slots):
            place = at[slots + t], at[2 * slots + t], at[3 * slots + t]
            both[place] += product(x[at[t]], u[t])
        if with_corr:
            term = pair_sums(x, rest[0])
            for y in range(ys):
                both[0, y, splits, :, :vectors] = term
                both[1, y, splits, :, :vectors] = term
        own[...], other[...] = both[0], both[1]

    shape = (ys, each, vectors, size)
    return pl.pallas_call(
        kernel,
        out_shape=arrays(shape, shape),
        in_specs=[SMEM] + [VMEM] * (3 if with_corr else 2),
        out_specs=(VMEM, VMEM),
        scratch_shapes=[pltpu.VMEM((2,) + shape, jnp.float32)],
        compiler_params=PARAMS,
        cost_estimate=cost(blocks, vectors),
        name="lower",
    )(table, blocks, row_piece, *((start_piece,) if with_corr else ()))


def add_from_other(own, cores):
    def kernel(a, b, out):
        out[...] = a[...] + b[1 - lax.axis_index("core")]

    return pl.pallas_call(
        kernel, out_shape=arrays(own.shape)[0], in_specs=[VMEM] * 2, out_specs=VMEM,
        compiler_params=PARAMS, name="add_from_other",
    )(own, cores)


def own_copies(row_piece, prepared, splits, copies):
    _, vectors, size = row_piece.shape

    def kernel(piece, _, out):
        first = lax.axis_index("col") * splits
        for s in range(splits):
            block = piece[first + s]
            for i in range(copies):
                out[i, s] = block

    return pl.pallas_call(
        kernel, out_shape=arrays((copies, splits, vectors, size))[0],
        in_specs=[VMEM] * 2, out_specs=VMEM, compiler_params=PARAMS, name="own_copies",
    )(row_piece, prepared)


def group_part(row_got, col_got, scaled):
    splits = row_got.shape[1]

    def kernel(rows, cols, own, out):
        mine = lax.axis_index("split")
        for s in range(splits):
            total = rows[0, s]
            for j in range(1, rows.shape[0]):
                total += rows[j, s]
            for i in range(cols.shape[0]):
                total += cols[i, s]
            total += own[...] * jnp.where(mine == s, 1.0, 0.0).astype(jnp.float32)
            for k in range(splits):
                out[k, s] = total

    return pl.pallas_call(
        kernel, out_shape=arrays((splits,) + row_got.shape[1:])[0],
        in_specs=[VMEM] * 3, out_specs=VMEM, compiler_params=PARAMS, name="group_part",
    )(row_got, col_got, scaled)


def image_copies(parts, ys, cols):
    splits, _, vectors, size = parts.shape

    def kernel(p, col_out, row_out, own):
        for s in range(splits):
            total = p[0, s]
            for k in range(1, splits):
                total += p[k, s]
            for j in range(cols):
                col_out[j, s] = total
            for i in range(ys):
                row_out[i, s] = total
        own[...] = row_out[0, lax.axis_index("split")]

    return pl.pallas_call(
        kernel,
        out_shape=arrays((cols, splits, vectors, size), (ys, splits, vectors, size), (vectors, size)),
        in_specs=[VMEM], out_specs=(VMEM,) * 3, compiler_params=PARAMS, name="image_copies",
    )(parts)


def add_to_messages(col_got, row_out):
    rows, more, vectors, size = col_got.shape
    splits = more - 1

    def kernel(got, sums, out, corr):
        out[...] = sums[...]
        first = lax.axis_index("col") * splits
        for s in range(more):
            total = got[0, s]
            for i in range(1, rows):
                total += got[i, s]
            if s < splits:
                out[first + s] += total
            else:
                corr[...] = total

    return pl.pallas_call(
        kernel, out_shape=arrays(row_out.shape, (vectors, size)),
        in_specs=[VMEM, VMEM], out_specs=(VMEM, VMEM), compiler_params=PARAMS,
        name="add_to_messages",
    )(col_got, row_out)


def subtract(corr, base, value, total):
    scaled = corr[:, : value.shape[0]] * (1.0 / total)
    return base - lax.dot_general(
        scaled, value, (((1,), (0,)), ((), ())), precision=HIGHEST,
        preferred_element_type=jnp.float32,
    )


def residual_of(corr, first, start, total):
    def kernel(c, f, v, out):
        out[...] = subtract(c[...], f[...], v[...], total)

    return pl.pallas_call(
        kernel, out_shape=arrays(first.shape)[0], in_specs=[VMEM] * 3, out_specs=VMEM,
        compiler_params=PARAMS, name="residual",
    )(corr, first, start)


def second_of(got, corr, first, diag, total):
    def kernel(g, c, f, d, out):
        value = f[...]
        image = d[...] * value
        for k in range(g.shape[0]):
            image += g[k]
        out[...] = subtract(c[...], image, value, total)

    return pl.pallas_call(
        kernel, out_shape=arrays(first.shape)[0], in_specs=[VMEM] * 4, out_specs=VMEM,
        compiler_params=PARAMS, name="second",
    )(got, corr, first, diag)


def exchange(parts, axis):
    return lax.all_to_all(parts, axis, 0, 0, tiled=True)


def both_cores(piece):
    return lax.all_gather(piece, "core", axis=0, tiled=False)


def on_device(start_vectors, diag_energy, matrix_blocks, block_rows, block_cols, counts):
    ys, cols, splits = (lax.axis_size(a) for a in ("y", "col", "split"))
    vectors, size = start_vectors.shape
    slots = matrix_blocks.shape[2]
    blocks = matrix_blocks.reshape(slots, size, size)
    row_ids = block_rows.reshape(slots)
    col_ids = block_cols.reshape(slots)
    count = counts.reshape(1)
    diag = diag_energy.reshape(1, size)
    total = size * ys * 2 * cols * splits
    plane = ("col", "split")

    start_row = exchange(start_copies(start_vectors, cols * splits), plane)
    lower, upper, table, scaled = prepare(
        row_ids, col_ids, count, blocks, start_vectors, diag, splits
    )
    own_cols = exchange(own_copies(start_row, scaled, splits, ys), "y")
    own, other = lower_products(table, lower, start_row, None, ys, splits)
    col_got = exchange(add_from_other(own, both_cores(other)), "y")
    rows = upper_products(table, upper, both_cores(own_cols), cols * splits)
    row_got = exchange(rows.reshape(cols, splits, vectors, size), "col")
    parts = exchange(group_part(row_got, col_got, scaled), "split")

    col_copies, y_copies, first = image_copies(parts, ys, cols)
    first_row = exchange(col_copies, "col").reshape(cols * splits, vectors, size)
    own_cols = exchange(y_copies, "y")
    own, other = lower_products(table, lower, first_row, start_row, ys, splits)
    col_got = exchange(add_from_other(own, both_cores(other)), "y")
    rows = upper_products(table, upper, both_cores(own_cols), cols * splits)
    messages, corr = add_to_messages(col_got, rows)
    got = exchange(messages, plane)
    residual = residual_of(corr, first, start_vectors, total)
    return residual, second_of(got, corr, first, diag, total)


def solution(mesh):
    rows, cols, splits = mesh.devices.shape
    axes = ("y", "core", "col", "split")
    mesh = jax.sharding.Mesh(mesh.devices.reshape(rows // 2, 2, cols, splits), axes)
    row = ("y", "core")
    in_specs = (
        P(None, axes),
        P(axes),
        P(row, "col", "split", None, None),
        P(row, "col", "split"),
        P(row, "col", "split"),
        P(row, "col", "split"),
    )
    out_specs = (P(None, axes), P(None, axes))
    return jax.shard_map(
        on_device, mesh=mesh, in_specs=in_specs, out_specs=out_specs, check_vma=False
    )
```

```python
import jax
import jax.numpy as jnp
from jax import lax
from jax.experimental import pallas as pl
from jax.experimental.pallas import tpu as pltpu
from jax.sharding import PartitionSpec as P

HIGHEST = lax.Precision.HIGHEST
SMEM = pl.BlockSpec(memory_space=pltpu.SMEM)
VMEM = pl.BlockSpec(memory_space=pltpu.VMEM)
PARAMS = pltpu.CompilerParams(vmem_limit_bytes=16 << 20)


def arrays(*shapes):
    return tuple(jax.ShapeDtypeStruct(s, jnp.float32) for s in shapes)


def halves(x):
    high = x.astype(jnp.bfloat16)
    return high, (x - high.astype(jnp.float32)).astype(jnp.bfloat16)


def prepare(row_ids, col_ids, count, blocks, start, diag, splits):
    slots, size, _ = blocks.shape

    def kernel(r, c, n, u, v, d, lower, upper, table, scaled, own_start, own_diag):
        core = lax.axis_index("core")
        for t in range(slots):
            row, split = lax.div(c[t], jnp.int32(splits)), lax.rem(c[t], jnp.int32(splits))
            table[t] = r[t]
            table[slots + t] = jnp.where(lax.rem(row, jnp.int32(2)) == core, 0, 1)
            table[2 * slots + t] = lax.div(row, jnp.int32(2))
            table[3 * slots + t] = split
            table[4 * slots + t] = lax.rem(row, jnp.int32(2))
            block = u[t] * jnp.where(t < n[0], 1.0, 0.0).astype(jnp.float32)
            for out, x in ((lower, block), (upper, block.T)):
                high, low = halves(x)
                out[t, :, :size] = high
                out[t, :, size:] = low
        scaled[...] = v[...] * d[...]
        own_start[...] = v[...]
        own_diag[...] = jnp.broadcast_to(d[...], v.shape)

    both = jax.ShapeDtypeStruct((slots, size, 2 * size), jnp.bfloat16)
    return pl.pallas_call(
        kernel,
        out_shape=(
            both, both, jax.ShapeDtypeStruct((5 * slots,), jnp.int32),
            *arrays(*[start.shape] * 3),
        ),
        in_specs=[SMEM] * 3 + [VMEM] * 3,
        out_specs=(VMEM, VMEM, SMEM, VMEM, VMEM, VMEM),
        compiler_params=PARAMS,
        cost_estimate=pl.CostEstimate(
            flops=8 * blocks.size, bytes_accessed=12 * blocks.size, transcendentals=0
        ),
        name="prepare",
    )(row_ids, col_ids, count, blocks, start, diag)


def product(x, block):
    rows, size = x.shape
    high = x.astype(jnp.bfloat16).astype(jnp.float32)
    pair = jnp.concatenate([high, x - high], 0).astype(jnp.bfloat16)
    terms = lax.dot_general(
        pair, block, (((1,), (0,)), ((), ())), preferred_element_type=jnp.float32
    )
    terms = terms[:rows] + terms[rows:]
    return terms[:, :size] + terms[:, size:]


def pair_sums(one, two):
    blocks, vectors, size = one.shape
    sums = [jnp.zeros((vectors, size), jnp.float32) for _ in range(vectors)]
    for g in range(blocks):
        x, v = one[g], two[g]
        for r in range(vectors):
            sums[r] += x * (pltpu.roll(v, r, 0) if r else v)
    l = lax.broadcasted_iota(jnp.int32, (vectors, vectors), 0)
    k = lax.broadcasted_iota(jnp.int32, (vectors, vectors), 1)
    out = jnp.zeros((vectors, vectors), jnp.float32)
    for r in range(vectors):
        its = (l - k == r) | (l - k == r - vectors)
        out += jnp.where(its, jnp.sum(sums[r], axis=1, keepdims=True), 0.0)
    return out


def cost(blocks, vectors):
    return pl.CostEstimate(
        flops=4 * blocks.size * vectors, bytes_accessed=2 * blocks.size, transcendentals=0
    )


def start_copies(start, copies):
    def kernel(v, out):
        block = v[...]
        for i in range(copies):
            out[i] = block

    return pl.pallas_call(
        kernel, out_shape=arrays((copies,) + start.shape)[0], in_specs=[VMEM], out_specs=VMEM,
        compiler_params=PARAMS, name="start_copies",
    )(start)


def upper_products(table, blocks, cols, row_blocks):
    _, _, _, vectors, size = cols.shape
    slots = blocks.shape[0]

    def kernel(at, u, x, out):
        out[...] = jnp.zeros_like(out)
        for t in range(slots):
            place = at[4 * slots + t], at[2 * slots + t], at[3 * slots + t]
            out[at[t]] += product(x[place], u[t])

    return pl.pallas_call(
        kernel,
        out_shape=arrays((row_blocks, vectors, size))[0],
        in_specs=[SMEM] + [VMEM] * 2,
        out_specs=VMEM,
        compiler_params=PARAMS,
        cost_estimate=cost(blocks, vectors),
        name="upper",
    )(table, blocks, cols)


def lower_products(table, blocks, row_piece, start_piece, ys, splits):
    _, vectors, size = row_piece.shape
    slots = blocks.shape[0]
    with_corr = start_piece is not None
    each = splits + 1 if with_corr else splits

    def kernel(at, u, x, *rest):
        own, other, both = rest[-3:]
        both[...] = jnp.zeros_like(both)
        for t in range(slots):
            place = at[slots + t], at[2 * slots + t], at[3 * slots + t]
            both[place] += product(x[at[t]], u[t])
        if with_corr:
            term = pair_sums(x, rest[0])
            for y in range(ys):
                both[0, y, splits, :, :vectors] = term
                both[1, y, splits, :, :vectors] = term
        own[...], other[...] = both[0], both[1]

    shape = (ys, each, vectors, size)
    return pl.pallas_call(
        kernel,
        out_shape=arrays(shape, shape),
        in_specs=[SMEM] + [VMEM] * (3 if with_corr else 2),
        out_specs=(VMEM, VMEM),
        scratch_shapes=[pltpu.VMEM((2,) + shape, jnp.float32)],
        compiler_params=PARAMS,
        cost_estimate=cost(blocks, vectors),
        name="lower",
    )(table, blocks, row_piece, *((start_piece,) if with_corr else ()))


def add_from_other(own, cores):
    def kernel(a, b, out):
        out[...] = a[...] + b[1 - lax.axis_index("core")]

    return pl.pallas_call(
        kernel, out_shape=arrays(own.shape)[0], in_specs=[VMEM] * 2, out_specs=VMEM,
        compiler_params=PARAMS, name="add_from_other",
    )(own, cores)


def own_copies(row_piece, prepared, splits, copies):
    _, vectors, size = row_piece.shape

    def kernel(piece, _, out):
        first = lax.axis_index("col") * splits
        for s in range(splits):
            block = piece[first + s]
            for i in range(copies):
                out[i, s] = block

    return pl.pallas_call(
        kernel, out_shape=arrays((copies, splits, vectors, size))[0],
        in_specs=[VMEM] * 2, out_specs=VMEM, compiler_params=PARAMS, name="own_copies",
    )(row_piece, prepared)


def group_part(row_got, col_got, scaled):
    splits = row_got.shape[1]

    def kernel(rows, cols, own, out):
        mine = lax.axis_index("split")
        for s in range(splits):
            total = rows[0, s]
            for j in range(1, rows.shape[0]):
                total += rows[j, s]
            for i in range(cols.shape[0]):
                total += cols[i, s]
            total += own[...] * jnp.where(mine == s, 1.0, 0.0).astype(jnp.float32)
            for k in range(splits):
                out[k, s] = total

    return pl.pallas_call(
        kernel, out_shape=arrays((splits,) + row_got.shape[1:])[0],
        in_specs=[VMEM] * 3, out_specs=VMEM, compiler_params=PARAMS, name="group_part",
    )(row_got, col_got, scaled)


def image_copies(parts, ys, cols):
    splits, _, vectors, size = parts.shape

    def kernel(p, col_out, row_out, own):
        for s in range(splits):
            total = p[0, s]
            for k in range(1, splits):
                total += p[k, s]
            for j in range(cols):
                col_out[j, s] = total
            for i in range(ys):
                row_out[i, s] = total
        own[...] = row_out[0, lax.axis_index("split")]

    return pl.pallas_call(
        kernel,
        out_shape=arrays((cols, splits, vectors, size), (ys, splits, vectors, size), (vectors, size)),
        in_specs=[VMEM], out_specs=(VMEM,) * 3, compiler_params=PARAMS, name="image_copies",
    )(parts)


def add_to_messages(col_got, row_out):
    rows, more, vectors, size = col_got.shape
    splits = more - 1

    def kernel(got, sums, out, corr):
        out[...] = sums[...]
        first = lax.axis_index("col") * splits
        for s in range(more):
            total = got[0, s]
            for i in range(1, rows):
                total += got[i, s]
            if s < splits:
                out[first + s] += total
            else:
                corr[...] = total

    return pl.pallas_call(
        kernel, out_shape=arrays(row_out.shape, (vectors, size)),
        in_specs=[VMEM, VMEM], out_specs=(VMEM, VMEM), compiler_params=PARAMS,
        name="add_to_messages",
    )(col_got, row_out)


def subtract(corr, base, value, total):
    scaled = corr[:, : value.shape[0]] * (1.0 / total)
    return base - lax.dot_general(
        scaled, value, (((1,), (0,)), ((), ())), precision=HIGHEST,
        preferred_element_type=jnp.float32,
    )


def results(got, corr, first, start, diag, total):
    def kernel(g, c, f, v, d, residual, second):
        value = f[...]
        image = d[...] * value
        for k in range(g.shape[0]):
            image += g[k]
        residual[...] = subtract(c[...], value, v[...], total)
        second[...] = subtract(c[...], image, value, total)

    return pl.pallas_call(
        kernel, out_shape=arrays(first.shape, first.shape), in_specs=[VMEM] * 5,
        out_specs=(VMEM, VMEM), compiler_params=PARAMS, name="results",
    )(got, corr, first, start, diag)


def exchange(parts, axis):
    return lax.all_to_all(parts, axis, 0, 0, tiled=True)


def both_cores(piece):
    return lax.all_gather(piece, "core", axis=0, tiled=False)


def on_device(start_vectors, diag_energy, matrix_blocks, block_rows, block_cols, counts):
    ys, cols, splits = (lax.axis_size(a) for a in ("y", "col", "split"))
    vectors, size = start_vectors.shape
    slots = matrix_blocks.shape[2]
    blocks = matrix_blocks.reshape(slots, size, size)
    row_ids = block_rows.reshape(slots)
    col_ids = block_cols.reshape(slots)
    count = counts.reshape(1)
    diag = diag_energy.reshape(1, size)
    total = size * ys * 2 * cols * splits
    plane = ("col", "split")

    start_row = exchange(start_copies(start_vectors, cols * splits), plane)
    lower, upper, table, scaled, own_start, own_diag = prepare(
        row_ids, col_ids, count, blocks, start_vectors, diag, splits
    )
    own_cols = exchange(own_copies(start_row, scaled, splits, ys), "y")
    own, other = lower_products(table, lower, start_row, None, ys, splits)
    col_got = exchange(add_from_other(own, both_cores(other)), "y")
    rows = upper_products(table, upper, both_cores(own_cols), cols * splits)
    row_got = exchange(rows.reshape(cols, splits, vectors, size), "col")
    parts = exchange(group_part(row_got, col_got, scaled), "split")

    col_copies, y_copies, first = image_copies(parts, ys, cols)
    first_row = exchange(col_copies, "col").reshape(cols * splits, vectors, size)
    own_cols = exchange(y_copies, "y")
    own, other = lower_products(table, lower, first_row, start_row, ys, splits)
    col_got = exchange(add_from_other(own, both_cores(other)), "y")
    rows = upper_products(table, upper, both_cores(own_cols), cols * splits)
    messages, corr = add_to_messages(col_got, rows)
    got = exchange(messages, plane)
    return results(got, corr, first, own_start, own_diag, total)


def solution(mesh):
    rows, cols, splits = mesh.devices.shape
    axes = ("y", "core", "col", "split")
    mesh = jax.sharding.Mesh(mesh.devices.reshape(rows // 2, 2, cols, splits), axes)
    row = ("y", "core")
    in_specs = (
        P(None, axes),
        P(axes),
        P(row, "col", "split", None, None),
        P(row, "col", "split"),
        P(row, "col", "split"),
        P(row, "col", "split"),
    )
    out_specs = (P(None, axes), P(None, axes))
    return jax.shard_map(
        on_device, mesh=mesh, in_specs=in_specs, out_specs=out_specs, check_vma=False
    )
```
